32 devices in a mesh: dp: 8 (over y, x, core), mp: 4 (over z).
Axes of the slice: x: 2, y: 2, z: 4, core: 2. Of those that a mesh axis runs over, the one named last changes fastest.
Arguments:
- tokens: bfloat16 [2048, 32768], P('dp', 'mp'), may hold values from -6 to 6
- block_weights: bfloat16 [128, 8, 256, 256], P('mp'), may hold values from -0.125 to 0.125
- lowrank_down: bfloat16 [32768, 256], P(('mp', 'dp')), may hold values from -0.03125 to 0.03125
- lowrank_up: bfloat16 [32768, 256], P(('mp', 'dp')), may hold values from -0.375 to 0.375
- cotangent: bfloat16 [2048, 32768], P('dp', 'mp'), may hold values from -6 to 6
- seq_lengths: int32 [8], P('dp'), may hold values from 64 to 256, as said below
Outputs:
- output: bfloat16 [2048, 32768], P('dp', 'mp')
- grad_tokens: bfloat16 [2048, 32768], P('dp', 'mp')
- grad_blocks: bfloat16 [128, 8, 256, 256], P(('mp', 'dp'))
- grad_lowrank: bfloat16 [32768, 2, 256], P(('mp', 'dp'))
The draws below stay inside these ranges and needn't reach their ends.
Inputs may be any that keep to these rules, and one draw needn't show every extreme that they name: `seq_lengths`: each data shard holds one sequence in 256 slots, live from the first slot; some shard is full and some shard holds exactly 64 live tokens.
All inputs are finite; a program needn't handle non-finite values.
Results may differ from the reference program's by a relative error of at most 0.025.
Values may be sent and summed in bfloat16 or wider, within the bound.
A program may use at most 256 MiB of HBM per device.

```python
import jax
import jax.numpy as jnp
import numpy as np
from jax import lax

W = 32768
BLOCK = 256
LEVELS = 8
RANK = 256
TOK_DEV = 256
TOKENS = 2048
BLOCKS = 128
N_DP = 8


def draw_seq_lengths(key, part):
    first_key, second_key = jax.random.split(jax.random.fold_in(key, 7))
    lengths = jax.random.randint(first_key, (N_DP,), TOK_DEV // 4, TOK_DEV + 1)
    order = jax.random.permutation(second_key, N_DP)
    lengths = lengths.at[order[0]].set(TOK_DEV)
    lengths = lengths.at[order[1]].set(TOK_DEV // 4)
    return lengths.astype(jnp.int32)


def level_of(key, dims, cuts, smallest, high):
    level = 1.0
    for dim, blocks in cuts:
        heights = jax.random.uniform(jax.random.fold_in(jax.random.fold_in(key, 6), dim), (blocks,), jnp.float32, smallest / len(cuts), high / len(cuts))
        level = level * jnp.repeat(jnp.exp(heights), dims[dim] // blocks).reshape((-1,) + (1,) * (len(dims) - 1 - dim))
    return level


def noise(own_key, extent, deviation, limit, cuts=(), kind=jnp.bfloat16):
    drawn = deviation * jax.random.normal(own_key, extent, jnp.float32)
    if cuts:
        drawn = drawn * level_of(own_key, extent, cuts, -0.22, 0.18)
    return jnp.clip(drawn, -limit, limit).astype(kind)


def setup_inputs(seed: int = 0) -> dict:
    arg_keys = jax.random.split(jax.random.key(seed), 7)
    return {
        "tokens": noise(arg_keys[0], (TOKENS, W), 1.0, 6.0, ((0, 8), (1, 4))),
        "block_weights": noise(arg_keys[1], (BLOCKS, LEVELS, BLOCK, BLOCK), (LEVELS * BLOCK) ** -0.5, 0.125, ((0, 4),)),
        "lowrank_down": noise(arg_keys[2], (W, RANK), W ** -0.5, 0.03125, ((0, 32),)),
        "lowrank_up": noise(arg_keys[3], (W, RANK), RANK ** -0.5, 0.375, ((0, 32),)),
        "cotangent": noise(arg_keys[4], (TOKENS, W), 1.0, 6.0, ((0, 8), (1, 4))),
        "seq_lengths": draw_seq_lengths(jax.random.fold_in(arg_keys[6], 71), 0),
    }


def activate(values):
    return jax.nn.gelu(values, approximate=True)

def reference(tokens, block_weights, lowrank_down, lowrank_up, cotangent, seq_lengths):
    block_count = W // BLOCK
    table_np = np.array([[index if level == 0 else index ^ 1 << level - 1 for level in range(LEVELS)] for index in range(block_count)], dtype=np.int32)
    table = jnp.asarray(table_np)
    slot_ids = jnp.arange(TOKENS, dtype=jnp.int32)
    position = slot_ids % TOK_DEV
    shard_ids = slot_ids // TOK_DEV
    live = (position < seq_lengths[shard_ids]).astype(jnp.float32)[:, None]
    tok_blocks = tokens.reshape(TOKENS, block_count, BLOCK)
    down_proj = jnp.dot(tokens, lowrank_down, preferred_element_type=jnp.float32).astype(jnp.bfloat16)
    block_iota = jnp.arange(block_count, dtype=jnp.int32)
    level_iota = jnp.arange(LEVELS, dtype=jnp.int32)

    def forward_block(index):
        gathered = jnp.take(tok_blocks, table[index], axis=1).reshape(TOKENS, LEVELS * BLOCK)
        return jnp.dot(gathered, block_weights[index].reshape(LEVELS * BLOCK, BLOCK), preferred_element_type=jnp.float32)
    butterfly = lax.map(forward_block, block_iota)
    hidden = jnp.transpose(butterfly, (1, 0, 2)).reshape(TOKENS, W)
    hidden = hidden + jnp.dot(down_proj, lowrank_up.T, preferred_element_type=jnp.float32)
    output = (live * activate(hidden)).astype(jnp.bfloat16)
    _, pullback = jax.vjp(activate, hidden)
    pre_grad, = pullback(live * cotangent.astype(jnp.float32))
    grad_hidden = pre_grad.astype(jnp.bfloat16)
    up_proj = jnp.dot(grad_hidden, lowrank_up, preferred_element_type=jnp.float32).astype(jnp.bfloat16)
    hid_blocks = grad_hidden.reshape(TOKENS, block_count, BLOCK)

    def backward_block(index):
        sources = table[index]
        incoming = jnp.take(hid_blocks, sources, axis=1).astype(jnp.float32)
        matrices = block_weights[sources, level_iota].astype(jnp.float32)
        terms = jnp.einsum('tld,lcd->tlc', incoming, matrices).astype(jnp.bfloat16)
        terms = lax.optimization_barrier(terms)
        return lax.optimization_barrier(jnp.sum(terms.astype(jnp.float32), axis=1))
    back = lax.map(backward_block, block_iota)
    grad_tokens = jnp.transpose(back, (1, 0, 2)).reshape(TOKENS, W)
    grad_tokens = (grad_tokens + jnp.dot(up_proj, lowrank_down.T, preferred_element_type=jnp.float32)).astype(jnp.bfloat16)

    def weight_block(index):
        gathered = jnp.take(tok_blocks, table[index], axis=1).reshape(N_DP, TOK_DEV, LEVELS * BLOCK).astype(jnp.float32)
        hid_part = hid_blocks[:, index].reshape(N_DP, TOK_DEV, BLOCK).astype(jnp.float32)
        shard_grad = jnp.einsum('stc,std->scd', gathered, hid_part).astype(jnp.bfloat16)
        shard_grad = lax.optimization_barrier(shard_grad)
        return lax.optimization_barrier(jnp.sum(shard_grad.astype(jnp.float32), axis=0)).astype(jnp.bfloat16).reshape(LEVELS, BLOCK, BLOCK)
    grad_blocks = lax.map(weight_block, block_iota)

    def factor_shard(carry, pieces):
        tok_part, hid_part, down_part, up_part = pieces
        grad_down = jnp.dot(tok_part.T, up_part, preferred_element_type=jnp.float32)
        grad_up = jnp.dot(hid_part.T, down_part, preferred_element_type=jnp.float32)
        shard_factor = jnp.stack([grad_down, grad_up], axis=1).astype(jnp.bfloat16)
        shard_factor = lax.optimization_barrier(shard_factor)
        return (carry + shard_factor.astype(jnp.float32), None)
    initial = jnp.zeros((W, 2, RANK), jnp.float32)
    pieces = (tokens.reshape(N_DP, TOK_DEV, W), grad_hidden.reshape(N_DP, TOK_DEV, W), down_proj.reshape(N_DP, TOK_DEV, RANK), up_proj.reshape(N_DP, TOK_DEV, RANK))
    summed, _ = lax.scan(factor_shard, initial, pieces)
    grad_lowrank = summed.astype(jnp.bfloat16)
    return (output, grad_tokens, grad_blocks, grad_lowrank)
```

```python
import functools
import math

import jax
import jax.numpy as jnp
from jax import lax
from jax.experimental import pallas as pl
from jax.experimental.pallas import tpu as pltpu
from jax.sharding import PartitionSpec as P

F32 = jnp.float32
BF16 = jnp.bfloat16
VMEM_LIMIT = 48 * 2**20


def partner(value, axis, mask):
    pairs = [(source, source ^ mask) for source in range(lax.axis_size(axis))]
    return lax.ppermute(value, axis, pairs)


def dot(lhs, rhs, left, right):
    return lax.dot_general(lhs, rhs, (((left,), (right,)), ((), ())), preferred_element_type=F32)


def mp_sum(part):
    total = part.astype(F32)
    for mask in range(1, lax.axis_size("mp")):
        total = total + partner(part, "mp", mask).astype(F32)
    return total.astype(BF16)


def forward_kernel(n_local, n_remote, has_prev, seq_ref, *refs):
    levels = n_local + n_remote
    sources = refs[:levels]
    w_ref, up_ref, down_ref, cot_ref = refs[levels : levels + 4]
    outs = refs[levels + 4 + (2 if has_prev else 0) :]
    out_ref, g_ref, wgrad_ref, upsum_ref = outs[:4]
    term_refs = outs[4:]
    hidden = dot(down_ref[...], up_ref[...], 1, 1)
    for level in range(levels):
        hidden = hidden + dot(sources[level][...], w_ref[0, level], 1, 0)
    rows = lax.broadcasted_iota(jnp.int32, hidden.shape, 0)
    live = rows < seq_ref[0]
    root = math.sqrt(2.0 / math.pi)
    square = hidden * hidden
    slope = jnp.tanh(root * hidden * (1.0 + 0.044715 * square))
    cdf = 0.5 + 0.5 * slope
    out_ref[...] = jnp.where(live, hidden * cdf, 0.0).astype(BF16)
    deriv = cdf + (0.5 * root) * hidden * (1.0 - slope * slope) * (1.0 + (3 * 0.044715) * square)
    grad = jnp.where(live, cot_ref[...].astype(F32) * deriv, 0.0).astype(BF16)
    g_ref[...] = grad
    for index, term_ref in enumerate(term_refs):
        term_ref[...] = dot(grad, w_ref[0, n_local + index], 1, 1).astype(BF16)
    for level in range(levels):
        wgrad_ref[0, level] = dot(sources[level][...], grad, 0, 0).astype(BF16)

    @pl.when((pl.program_id(0) == 0) & (pl.program_id(1) == 0))
    def _():
        upsum_ref[...] = jnp.zeros_like(upsum_ref)

    upsum_ref[...] += dot(grad, up_ref[...], 1, 0)


def forward_chunk(
    chunk, sizes, seq, tokens, remote, weights, up_factor, down_sum, cotangent, prev, extra
):
    dp, quota, per, n_local, blk = sizes
    rows, features = tokens.shape
    rank = down_sum.shape[1]
    levels = weights.shape[1]

    def block(d, s):
        return d * quota + chunk * per + s

    def local_spec(mask):
        return pl.BlockSpec((rows, blk), lambda d, s: (0, block(d, s) ^ mask))

    masks = [0] + [2**bit for bit in range(n_local - 1)]
    packed_spec = pl.BlockSpec((rows, blk), lambda d, s: (0, d * per + s))
    any_spec = pl.BlockSpec(memory_space=pl.ANY)
    in_specs = (
        [pl.BlockSpec(memory_space=pltpu.SMEM)]
        + [local_spec(mask) for mask in masks]
        + [packed_spec for _ in remote]
        + [
            pl.BlockSpec((1, levels, blk, blk), lambda d, s: (block(d, s), 0, 0, 0)),
            pl.BlockSpec((blk, rank), lambda d, s: (block(d, s), 0)),
            pl.BlockSpec((rows, rank), lambda d, s: (0, 0)),
            local_spec(0),
        ]
        + [any_spec for _ in prev]
    )
    args = [seq] + [tokens for _ in masks] + list(remote)
    args += [weights, up_factor, down_sum, cotangent] + list(prev)
    aliases = {len(args) - 2: 0, len(args) - 1: 1} if prev else {}
    wide = jax.ShapeDtypeStruct((rows, features), BF16)
    packed = jax.ShapeDtypeStruct((rows, dp * per * blk), BF16)
    steps = dp * per
    return pl.pallas_call(
        functools.partial(forward_kernel, n_local, len(remote), bool(prev)),
        grid=(dp, per),
        in_specs=in_specs,
        out_specs=[
            local_spec(0),
            local_spec(0),
            pl.BlockSpec((1, levels, blk, blk), lambda d, s: (d, s, 0, 0)),
            pl.BlockSpec((rows, rank), lambda d, s: (0, 0)),
        ]
        + [packed_spec for _ in remote],
        out_shape=[
            wide,
            wide,
            jax.ShapeDtypeStruct((dp, per * levels + extra, blk, blk), BF16),
            jax.ShapeDtypeStruct((rows, rank), F32),
        ]
        + [packed for _ in remote],
        input_output_aliases=aliases,
        compiler_params=pltpu.CompilerParams(vmem_limit_bytes=VMEM_LIMIT),
        cost_estimate=pl.CostEstimate(
            flops=steps * 22 * 2 * rows * blk * blk,
            bytes_accessed=steps * 4 * 2**20,
            transcendentals=steps * rows * blk,
        ),
        name="forward_%d" % chunk,
    )(*args)


def factor_kernel(tok_ref, g_ref, up_ref, down_ref, buf_ref, out_ref):
    out_ref[0, 0] = dot(tok_ref[...], up_ref[...], 0, 0).astype(BF16)
    out_ref[0, 1] = dot(g_ref[...], down_ref[...], 0, 0).astype(BF16)


def factor_grads(sizes, tokens, grad_hidden, up_sum, down_sum, buffer, offset):
    dp, quota, per, n_local, blk = sizes
    rows = tokens.shape[0]
    rank = up_sum.shape[1]
    col = pl.BlockSpec((rows, blk), lambda d, s: (0, d * quota + s))
    whole = pl.BlockSpec((rows, rank), lambda d, s: (0, 0))
    return pl.pallas_call(
        factor_kernel,
        grid=(dp, quota),
        in_specs=[col, col, whole, whole, pl.BlockSpec(memory_space=pl.ANY)],
        out_specs=pl.BlockSpec((1, 2, blk, rank), lambda d, s: (d, offset // 2 + s, 0, 0)),
        out_shape=jax.ShapeDtypeStruct(buffer.shape, BF16),
        input_output_aliases={4: 0},
        compiler_params=pltpu.CompilerParams(vmem_limit_bytes=VMEM_LIMIT),
        cost_estimate=pl.CostEstimate(
            flops=dp * quota * 4 * rows * blk * rank,
            bytes_accessed=dp * quota * 2**19,
            transcendentals=0,
        ),
        name="factor_grads",
    )(tokens, grad_hidden, up_sum, down_sum, buffer)


def backward_kernel(n_local, *refs):
    g_refs, w_refs = refs[:n_local], refs[n_local : 2 * n_local]
    up_ref, down_ref, out_ref = refs[2 * n_local :]
    total = dot(up_ref[...], down_ref[...], 1, 1)
    for level in range(n_local):
        total = total + dot(g_refs[level][...], w_refs[level][0, 0], 1, 1)
    out_ref[...] = total


def backward_local(sizes, grad_hidden, weights, up_sum, down_factor):
    dp, quota, per, n_local, blk = sizes
    rows, features = grad_hidden.shape
    rank = up_sum.shape[1]
    blocks = weights.shape[0]

    def g_spec(mask):
        return pl.BlockSpec((rows, blk), lambda j: (0, j ^ mask))

    def w_spec(mask, level):
        return pl.BlockSpec((1, 1, blk, blk), lambda j: (j ^ mask, level, 0, 0))

    masks = [0] + [2**bit for bit in range(n_local - 1)]
    return pl.pallas_call(
        functools.partial(backward_kernel, n_local),
        grid=(blocks,),
        in_specs=[g_spec(mask) for mask in masks]
        + [w_spec(mask, level) for level, mask in enumerate(masks)]
        + [
            pl.BlockSpec((rows, rank), lambda j: (0, 0)),
            pl.BlockSpec((blk, rank), lambda j: (j, 0)),
        ],
        out_specs=g_spec(0),
        out_shape=jax.ShapeDtypeStruct((rows, features), F32),
        compiler_params=pltpu.CompilerParams(vmem_limit_bytes=VMEM_LIMIT),
        cost_estimate=pl.CostEstimate(
            flops=blocks * (n_local + 1) * 2 * rows * blk * blk,
            bytes_accessed=blocks * 2 * 2**20,
            transcendentals=0,
        ),
        name="backward_local",
    )(*([grad_hidden] * n_local), *([weights] * n_local), up_sum, down_factor)


def finish_kernel(n_remote, *refs):
    total = refs[0][...]
    for term_ref in refs[1 : 1 + n_remote]:
        total = total + term_ref[...].astype(F32)
    refs[-1][...] = total.astype(BF16)


def finish_chunk(chunk, sizes, partial, landed, prev):
    dp, quota, per, n_local, blk = sizes
    rows, features = partial.shape
    width = per * blk
    chunks = quota // per
    spec = pl.BlockSpec((rows, width), lambda d: (0, d * chunks + chunk))
    packed_spec = pl.BlockSpec((rows, width), lambda d: (0, d))
    return pl.pallas_call(
        functools.partial(finish_kernel, len(landed)),
        grid=(dp,),
        in_specs=[spec]
        + [packed_spec for _ in landed]
        + [pl.BlockSpec(memory_space=pl.ANY) for _ in prev],
        out_specs=spec,
        out_shape=jax.ShapeDtypeStruct((rows, features), BF16),
        input_output_aliases={1 + len(landed): 0} if prev else {},
        compiler_params=pltpu.CompilerParams(vmem_limit_bytes=VMEM_LIMIT),
        cost_estimate=pl.CostEstimate(
            flops=dp * rows * width * 3,
            bytes_accessed=dp * rows * width * 10,
            transcendentals=0,
        ),
        name="finish_%d" % chunk,
    )(partial, *landed, *prev)


def per_device(tokens, block_weights, lowrank_down, lowrank_up, cotangent, seq_lengths):
    rows = tokens.shape[0]
    local_blocks, levels, blk = block_weights.shape[:3]
    rank = lowrank_down.shape[1]
    dp = lax.axis_size("dp")
    quota = local_blocks // dp
    chunks = 2 if quota % 2 == 0 else 1
    per = quota // chunks
    n_local = local_blocks.bit_length()
    remote_masks = [2**bit for bit in range(levels - n_local)]
    sizes = (dp, quota, per, n_local, blk)
    width = per * blk

    down_factor = lax.all_gather(lowrank_down, "dp", axis=0, tiled=True)
    up_factor = lax.all_gather(lowrank_up, "dp", axis=0, tiled=True)

    arrived = []
    for chunk in range(chunks):
        starts = [(d * chunks + chunk) * width for d in range(dp)]
        sent = jnp.concatenate([tokens[:, at : at + width] for at in starts], axis=1)
        if chunk:
            sent, arrived[-1] = lax.optimization_barrier((sent, arrived[-1]))
        arrived.append([partner(sent, "mp", mask) for mask in remote_masks])

    down_part = jnp.dot(tokens, down_factor, preferred_element_type=F32).astype(BF16)
    down_sum = mp_sum(down_part)

    prev = ()
    pending, wgrads = [], []
    up_part = None
    for chunk in range(chunks):
        last = chunk == chunks - 1
        out, grad_hidden, wgrad, up_chunk, *terms = forward_chunk(
            chunk,
            sizes,
            seq_lengths,
            tokens,
            arrived[chunk],
            block_weights,
            up_factor,
            down_sum,
            cotangent,
            prev,
            2 * quota if last else 0,
        )
        prev = (out, grad_hidden)
        up_part = up_chunk if up_part is None else up_part + up_chunk
        pending.append(terms)
        wgrads.append(wgrad)
        if not last:
            pending[-1], arrived[chunk + 1] = lax.optimization_barrier((terms, arrived[chunk + 1]))

    scattered = [
        lax.psum_scatter(wgrad, "dp", scatter_dimension=0, tiled=True) for wgrad in wgrads[:-1]
    ]
    up_sum = mp_sum(up_part.astype(BF16))
    returned = [
        [partner(term, "mp", mask) for term, mask in zip(terms, remote_masks)] for terms in pending
    ]
    merged = factor_grads(
        sizes, tokens, grad_hidden, up_sum, down_sum, wgrads[-1], per * levels
    )
    merged, scattered = lax.optimization_barrier((merged, scattered))
    scattered.append(lax.psum_scatter(merged, "dp", scatter_dimension=0, tiled=True))
    partial = backward_local(sizes, grad_hidden, block_weights, up_sum, down_factor)
    grad_tokens = ()
    for chunk in range(chunks):
        grad_tokens = (finish_chunk(chunk, sizes, partial, returned[chunk], grad_tokens),)

    pieces = [part[0, : per * levels] for part in scattered]
    grad_blocks = jnp.concatenate(pieces, axis=0).reshape(quota, levels, blk, blk)
    factors = scattered[-1][0, per * levels :].reshape(quota, 2, blk, rank)
    grad_lowrank = jnp.transpose(factors, (0, 2, 1, 3)).reshape(quota * blk, 2, rank)
    return (out, grad_tokens[0], grad_blocks, grad_lowrank)


def solution(mesh):
    placed = (
        P("dp", "mp"),
        P("mp", None, None, None),
        P(("mp", "dp"), None),
        P(("mp", "dp"), None),
        P("dp", "mp"),
        P("dp"),
    )
    return jax.shard_map(
        per_device,
        mesh=mesh,
        in_specs=placed,
        out_specs=(
            P("dp", "mp"),
            P("dp", "mp"),
            P(("mp", "dp"), None, None, None),
            P(("mp", "dp"), None, None),
        ),
        check_vma=False,
    )
```

```python
import functools
import math

import jax
import jax.numpy as jnp
from jax import lax
from jax.experimental import pallas as pl
from jax.experimental.pallas import tpu as pltpu
from jax.sharding import PartitionSpec as P

F32 = jnp.float32
BF16 = jnp.bfloat16
VMEM_LIMIT = 48 * 2**20


def partner(value, axis, mask):
    pairs = [(source, source ^ mask) for source in range(lax.axis_size(axis))]
    return lax.ppermute(value, axis, pairs)


def dot(lhs, rhs, left, right):
    return lax.dot_general(lhs, rhs, (((left,), (right,)), ((), ())), preferred_element_type=F32)


def mp_sum(part):
    total = part.astype(F32)
    for mask in range(1, lax.axis_size("mp")):
        total = total + partner(part, "mp", mask).astype(F32)
    return total.astype(BF16)


def forward_kernel(n_local, n_remote, has_prev, seq_ref, *refs):
    levels = n_local + n_remote
    sources = refs[:levels]
    turned = refs[levels : levels + n_local]
    refs = refs[levels + n_local :]
    w_ref, up_ref, down_ref, cot_ref = refs[:4]
    outs = refs[4 + (2 if has_prev else 0) :]
    out_ref, g_ref, wgrad_ref, upsum_ref = outs[:4]
    term_refs = outs[4:]
    hidden = dot(down_ref[...], up_ref[...], 1, 1)
    for level in range(levels):
        hidden = hidden + dot(sources[level][...], w_ref[0, level], 1, 0)
    rows = lax.broadcasted_iota(jnp.int32, hidden.shape, 0)
    live = rows < seq_ref[0]
    root = math.sqrt(2.0 / math.pi)
    square = hidden * hidden
    slope = jnp.tanh(root * hidden * (1.0 + 0.044715 * square))
    cdf = 0.5 + 0.5 * slope
    out_ref[...] = jnp.where(live, hidden * cdf, 0.0).astype(BF16)
    deriv = cdf + (0.5 * root) * hidden * (1.0 - slope * slope) * (1.0 + (3 * 0.044715) * square)
    grad = jnp.where(live, cot_ref[...].astype(F32) * deriv, 0.0).astype(BF16)
    g_ref[...] = grad
    for index, term_ref in enumerate(term_refs):
        term_ref[...] = dot(grad, w_ref[0, n_local + index], 1, 1).astype(BF16)
    for level in range(levels):
        if level < n_local:
            product = dot(turned[level][...], grad, 1, 0)
        else:
            product = dot(sources[level][...], grad, 0, 0)
        wgrad_ref[0, level] = product.astype(BF16)

    @pl.when((pl.program_id(0) == 0) & (pl.program_id(1) == 0))
    def _():
        upsum_ref[...] = jnp.zeros_like(upsum_ref)

    upsum_ref[...] += dot(grad, up_ref[...], 1, 0)


def forward_chunk(
    chunk, sizes, seq, tokens, turned, remote, weights, up_factor, down_sum, cotangent, prev
):
    dp, quota, per, n_local, blk = sizes
    rows, features = tokens.shape
    rank = down_sum.shape[1]
    levels = weights.shape[1]

    def block(d, s):
        return d * quota + chunk * per + s

    def local_spec(mask):
        return pl.BlockSpec((rows, blk), lambda d, s: (0, block(d, s) ^ mask))

    def turned_spec(mask):
        return pl.BlockSpec((blk, rows), lambda d, s: (block(d, s) ^ mask, 0))

    masks = [0] + [2**bit for bit in range(n_local - 1)]
    packed_spec = pl.BlockSpec((rows, blk), lambda d, s: (0, d * per + s))
    any_spec = pl.BlockSpec(memory_space=pl.ANY)
    in_specs = (
        [pl.BlockSpec(memory_space=pltpu.SMEM)]
        + [local_spec(mask) for mask in masks]
        + [packed_spec for _ in remote]
        + [turned_spec(mask) for mask in masks]
        + [
            pl.BlockSpec((1, levels, blk, blk), lambda d, s: (block(d, s), 0, 0, 0)),
            pl.BlockSpec((blk, rank), lambda d, s: (block(d, s), 0)),
            pl.BlockSpec((rows, rank), lambda d, s: (0, 0)),
            local_spec(0),
        ]
        + [any_spec for _ in prev]
    )
    args = [seq] + [tokens for _ in masks] + list(remote) + [turned for _ in masks]
    args += [weights, up_factor, down_sum, cotangent] + list(prev)
    aliases = {len(args) - 2: 0, len(args) - 1: 1} if prev else {}
    wide = jax.ShapeDtypeStruct((rows, features), BF16)
    packed = jax.ShapeDtypeStruct((rows, dp * per * blk), BF16)
    steps = dp * per
    return pl.pallas_call(
        functools.partial(forward_kernel, n_local, len(remote), bool(prev)),
        grid=(dp, per),
        in_specs=in_specs,
        out_specs=[
            local_spec(0),
            local_spec(0),
            pl.BlockSpec((1, levels, blk, blk), lambda d, s: (d, s, 0, 0)),
            pl.BlockSpec((rows, rank), lambda d, s: (0, 0)),
        ]
        + [packed_spec for _ in remote],
        out_shape=[
            wide,
            wide,
            jax.ShapeDtypeStruct((dp, per * levels, blk, blk), BF16),
            jax.ShapeDtypeStruct((rows, rank), F32),
        ]
        + [packed for _ in remote],
        input_output_aliases=aliases,
        compiler_params=pltpu.CompilerParams(vmem_limit_bytes=VMEM_LIMIT),
        cost_estimate=pl.CostEstimate(
            flops=steps * 22 * 2 * rows * blk * blk,
            bytes_accessed=steps * 4 * 2**20,
            transcendentals=steps * rows * blk,
        ),
        name="forward_%d" % chunk,
    )(*args)


def factor_kernel(tok_ref, g_ref, up_ref, down_ref, out_ref):
    blk = out_ref.shape[2]
    for index in range(out_ref.shape[1] // 2):
        cols = pl.ds(index * blk, blk)
        out_ref[0, 2 * index] = dot(tok_ref[:, cols], up_ref[...], 0, 0).astype(BF16)
        out_ref[0, 2 * index + 1] = dot(g_ref[:, cols], down_ref[...], 0, 0).astype(BF16)


def factor_grads(sizes, tokens, grad_hidden, up_sum, down_sum):
    dp, quota, per, n_local, blk = sizes
    rows = tokens.shape[0]
    rank = up_sum.shape[1]
    col = pl.BlockSpec((rows, quota * blk), lambda d: (0, d))
    whole = pl.BlockSpec((rows, rank), lambda d: (0, 0))
    return pl.pallas_call(
        factor_kernel,
        grid=(dp,),
        in_specs=[col, col, whole, whole],
        out_specs=pl.BlockSpec((1, 2 * quota, blk, rank), lambda d: (d, 0, 0, 0)),
        out_shape=jax.ShapeDtypeStruct((dp, 2 * quota, blk, rank), BF16),
        compiler_params=pltpu.CompilerParams(vmem_limit_bytes=VMEM_LIMIT),
        cost_estimate=pl.CostEstimate(
            flops=dp * quota * 4 * rows * blk * rank,
            bytes_accessed=dp * quota * 2**19,
            transcendentals=0,
        ),
        name="factor_grads",
    )(tokens, grad_hidden, up_sum, down_sum)


def backward_kernel(n_local, *refs):
    g_refs, w_refs = refs[:n_local], refs[n_local : 2 * n_local]
    up_ref, down_ref, out_ref = refs[2 * n_local :]
    total = dot(up_ref[...], down_ref[...], 1, 1)
    for level in range(n_local):
        total = total + dot(g_refs[level][...], w_refs[level][0, 0], 1, 1)
    out_ref[...] = total


def backward_local(sizes, grad_hidden, weights, up_sum, down_factor):
    dp, quota, per, n_local, blk = sizes
    rows, features = grad_hidden.shape
    rank = up_sum.shape[1]
    blocks = weights.shape[0]

    def g_spec(mask):
        return pl.BlockSpec((rows, blk), lambda j: (0, j ^ mask))

    def w_spec(mask, level):
        return pl.BlockSpec((1, 1, blk, blk), lambda j: (j ^ mask, level, 0, 0))

    masks = [0] + [2**bit for bit in range(n_local - 1)]
    return pl.pallas_call(
        functools.partial(backward_kernel, n_local),
        grid=(blocks,),
        in_specs=[g_spec(mask) for mask in masks]
        + [w_spec(mask, level) for level, mask in enumerate(masks)]
        + [
            pl.BlockSpec((rows, rank), lambda j: (0, 0)),
            pl.BlockSpec((blk, rank), lambda j: (j, 0)),
        ],
        out_specs=g_spec(0),
        out_shape=jax.ShapeDtypeStruct((rows, features), F32),
        compiler_params=pltpu.CompilerParams(vmem_limit_bytes=VMEM_LIMIT),
        cost_estimate=pl.CostEstimate(
            flops=blocks * (n_local + 1) * 2 * rows * blk * blk,
            bytes_accessed=blocks * 2 * 2**20,
            transcendentals=0,
        ),
        name="backward_local",
    )(*([grad_hidden] * n_local), *([weights] * n_local), up_sum, down_factor)


def finish_kernel(n_remote, *refs):
    total = refs[0][...]
    for term_ref in refs[1 : 1 + n_remote]:
        total = total + term_ref[...].astype(F32)
    refs[-1][...] = total.astype(BF16)


def finish_chunk(chunk, sizes, partial, landed, prev):
    dp, quota, per, n_local, blk = sizes
    rows, features = partial.shape
    width = per * blk
    chunks = quota // per
    spec = pl.BlockSpec((rows, width), lambda d: (0, d * chunks + chunk))
    packed_spec = pl.BlockSpec((rows, width), lambda d: (0, d))
    return pl.pallas_call(
        functools.partial(finish_kernel, len(landed)),
        grid=(dp,),
        in_specs=[spec]
        + [packed_spec for _ in landed]
        + [pl.BlockSpec(memory_space=pl.ANY) for _ in prev],
        out_specs=spec,
        out_shape=jax.ShapeDtypeStruct((rows, features), BF16),
        input_output_aliases={1 + len(landed): 0} if prev else {},
        compiler_params=pltpu.CompilerParams(vmem_limit_bytes=VMEM_LIMIT),
        cost_estimate=pl.CostEstimate(
            flops=dp * rows * width * 3,
            bytes_accessed=dp * rows * width * 10,
            transcendentals=0,
        ),
        name="finish_%d" % chunk,
    )(partial, *landed, *prev)


def per_device(tokens, block_weights, lowrank_down, lowrank_up, cotangent, seq_lengths):
    rows = tokens.shape[0]
    local_blocks, levels, blk = block_weights.shape[:3]
    rank = lowrank_down.shape[1]
    dp = lax.axis_size("dp")
    quota = local_blocks // dp
    chunks = 2 if quota % 2 == 0 else 1
    per = quota // chunks
    n_local = local_blocks.bit_length()
    remote_masks = [2**bit for bit in range(levels - n_local)]
    sizes = (dp, quota, per, n_local, blk)
    width = per * blk

    down_factor = lax.all_gather(lowrank_down, "dp", axis=0, tiled=True)
    up_factor = lax.all_gather(lowrank_up, "dp", axis=0, tiled=True)

    turned = tokens.T
    arrived = []
    for chunk in range(chunks):
        starts = [(d * chunks + chunk) * width for d in range(dp)]
        sent = jnp.concatenate([tokens[:, at : at + width] for at in starts], axis=1)
        if chunk:
            sent, arrived[-1] = lax.optimization_barrier((sent, arrived[-1]))
        arrived.append([partner(sent, "mp", mask) for mask in remote_masks])

    down_part = jnp.dot(tokens, down_factor, preferred_element_type=F32).astype(BF16)
    down_sum = mp_sum(down_part)

    prev = ()
    pending, wgrads = [], []
    up_part = None
    for chunk in range(chunks):
        out, grad_hidden, wgrad, up_chunk, *terms = forward_chunk(
            chunk,
            sizes,
            seq_lengths,
            tokens,
            turned,
            arrived[chunk],
            block_weights,
            up_factor,
            down_sum,
            cotangent,
            prev,
        )
        prev = (out, grad_hidden)
        up_part = up_chunk if up_part is None else up_part + up_chunk
        pending.append(terms)
        wgrads.append(wgrad)
        if chunk < chunks - 1:
            pending[-1], arrived[chunk + 1] = lax.optimization_barrier((terms, arrived[chunk + 1]))

    scattered = []
    for wgrad in wgrads:
        if scattered:
            wgrad, scattered = lax.optimization_barrier((wgrad, scattered))
        scattered.append(lax.psum_scatter(wgrad, "dp", scatter_dimension=0, tiled=True))
    up_sum = mp_sum(up_part.astype(BF16))
    returned = [
        [partner(term, "mp", mask) for term, mask in zip(terms, remote_masks)] for terms in pending
    ]
    factors = factor_grads(sizes, tokens, grad_hidden, up_sum, down_sum)
    factors = lax.psum_scatter(factors, "dp", scatter_dimension=0, tiled=True)
    partial = backward_local(sizes, grad_hidden, block_weights, up_sum, down_factor)
    grad_tokens = ()
    for chunk in range(chunks):
        grad_tokens = (finish_chunk(chunk, sizes, partial, returned[chunk], grad_tokens),)

    grad_blocks = jnp.concatenate(scattered, axis=1).reshape(quota, levels, blk, blk)
    factors = factors.reshape(quota, 2, blk, rank)
    grad_lowrank = jnp.transpose(factors, (0, 2, 1, 3)).reshape(quota * blk, 2, rank)
    return (out, grad_tokens[0], grad_blocks, grad_lowrank)


def solution(mesh):
    placed = (
        P("dp", "mp"),
        P("mp", None, None, None),
        P(("mp", "dp"), None),
        P(("mp", "dp"), None),
        P("dp", "mp"),
        P("dp"),
    )
    return jax.shard_map(
        per_device,
        mesh=mesh,
        in_specs=placed,
        out_specs=(
            P("dp", "mp"),
            P("dp", "mp"),
            P(("mp", "dp"), None, None, None),
            P(("mp", "dp"), None, None),
        ),
        check_vma=False,
    )
```
